256 devices in a mesh: img: 16 (over z_lo, x, core), ref: 16 (over z_hi, y).
Axes of the slice: x: 4, y: 4, z: 8 (z_hi: 4, z_lo: 2; z = z_hi * 2 + z_lo), core: 2. Of those that a mesh axis runs over, the one named last changes fastest.
Arguments:
- images: bfloat16 [8192, 16384], P('img', 'ref'), may hold values from -24 to 24
- refs: bfloat16 [6912, 16384], P('ref', 'img'), may hold values from -0.0859375 to 0.0859375
- ctf: float32 [16, 16384], replicated, may hold values from 0.1 to 1
- ctf_group: int32 [8192], P('img'), may hold values from 0 to 15
- class_id: int32 [6912], P('ref'), may hold values from 0 to 191
- rot_id: int32 [6912], P('ref'), may hold values from 0 to 35
- class_prior: float32 [192], replicated, may hold values from -1 to 1
- rot_prior: float32 [36], replicated, may hold values from -1 to 1
Outputs:
- class_avg: float32 [192, 16384], P('img', 'ref')
- occupancy: float32 [192], replicated
- log_evidence: float32 [8192], P('img')
The draws below stay inside these ranges and needn't reach their ends.
All inputs are finite; a program needn't handle non-finite values.
Results may differ from the reference program's by a relative error of at most 0.0029.
Values may be sent and summed in bfloat16 or wider, within the bound.
No kernel may reach another device: no remote copies, remote signals or barrier semaphores. Data moves between devices by JAX's collectives and lax.ppermute only.
A program may use at most 128 MiB of HBM per device.

```python
import math
import jax
import jax.numpy as jnp
from jax import lax

FREQ = 16384
NCLASS = 192
NROT = 36
NGROUP = 16
NIMG = 8192
NREF = 6912


def shared_refs(key):
    spread = jax.random.uniform(jax.random.fold_in(key, 11), (NREF, 1), jnp.float32, -0.7, 0.7)
    noise = jnp.clip(jax.random.normal(jax.random.fold_in(key, 12), (NREF, FREQ), jnp.float32), -5.0, 5.0)
    return noise * jnp.exp(spread) / math.sqrt(FREQ)


def draw_refs(key, part):
    shared = shared_refs(key)
    return shared.astype(jnp.bfloat16)


def draw_images(key, part):
    key = jax.random.fold_in(key, 5)
    values = jax.random.normal(jax.random.fold_in(key, 1), (NIMG, FREQ), jnp.float32)
    return jnp.clip(values, -24.0, 24.0).astype(jnp.bfloat16)


def touch_ends(array, stream_key, smallest, largest):
    index_at = [jax.random.randint(jax.random.fold_in(stream_key, axis), (), 0, length) for axis, length in enumerate(array.shape)]
    main_axis = array.shape.index(max(array.shape))
    next_to = index_at[:main_axis] + [(index_at[main_axis] + 1) % array.shape[main_axis]] + index_at[main_axis + 1:]
    return array.at[tuple(index_at)].set(smallest).at[tuple(next_to)].set(largest)


def setup_inputs(seed: int = 0) -> dict:
    key_of = jax.random.split(jax.random.key(seed), 9)
    return {
        "images": draw_images(jax.random.fold_in(key_of[8], 71), 0),
        "refs": draw_refs(jax.random.fold_in(key_of[8], 71), 0),
        "ctf": jnp.clip(jax.random.uniform(key_of[2], (NGROUP, FREQ), jnp.float32, 0.1, 1.0), 0.1, 1.0),
        "ctf_group": touch_ends(jax.random.randint(key_of[3], (NIMG,), 0, NGROUP), jax.random.fold_in(key_of[3], 1), 0, NGROUP - 1).astype(jnp.int32),
        "class_id": touch_ends(jax.random.randint(key_of[4], (NREF,), 0, NCLASS), jax.random.fold_in(key_of[4], 1), 0, NCLASS - 1).astype(jnp.int32),
        "rot_id": touch_ends(jax.random.randint(key_of[5], (NREF,), 0, NROT), jax.random.fold_in(key_of[5], 1), 0, NROT - 1).astype(jnp.int32),
        "class_prior": jnp.clip(jax.random.uniform(key_of[6], (NCLASS,), jnp.float32, -1.0, 1.0), -1.0, 1.0),
        "rot_prior": jnp.clip(jax.random.uniform(key_of[7], (NROT,), jnp.float32, -1.0, 1.0), -1.0, 1.0),
    }


def reference(images, refs, ctf, ctf_group, class_id, rot_id, class_prior, rot_prior):
    highest = lax.Precision.HIGHEST
    ref_float = refs.astype(jnp.float32)
    ctf_square = ctf * ctf
    norms = jnp.dot(ctf_square, (ref_float * ref_float).T, precision=highest)
    priors = class_prior[class_id] + rot_prior[rot_id]
    offsets = priors[None, :] - 0.5 * norms
    weighted = (ctf[ctf_group] * images.astype(jnp.float32)).astype(jnp.bfloat16)
    class_hot = (class_id[:, None] == jnp.arange(NCLASS, dtype=jnp.int32)[None, :]).astype(jnp.float32)
    block_rows = min(512, NIMG)

    def one_block(inputs):
        image_block, group_block = inputs
        scores = jnp.dot(image_block, refs.T, preferred_element_type=jnp.float32) + offsets[group_block]
        row_top = jnp.max(scores, axis=1)
        row_sum = jnp.sum(jnp.exp(scores - row_top[:, None]), axis=1)
        evidence = row_top + jnp.log(row_sum)
        posterior = jnp.exp(scores - evidence[:, None])
        return evidence, jnp.dot(posterior, class_hot, precision=highest)

    evidence, class_post = lax.map(one_block, (weighted.reshape(-1, block_rows, FREQ), ctf_group.reshape(-1, block_rows)))
    evidence = evidence.reshape(NIMG)
    class_post = class_post.reshape(NIMG, NCLASS)
    counts = jnp.sum(class_post, axis=0)
    post_weights = class_post.astype(jnp.bfloat16)
    class_sums = jnp.dot(post_weights.T, images, preferred_element_type=jnp.float32)
    class_avg = class_sums / (counts[:, None] + 1.0)
    occupancy = counts * (NCLASS / NIMG)
    return class_avg, occupancy, evidence
```

```python
import jax
import jax.numpy as jnp
from jax import lax
from jax.sharding import Mesh, PartitionSpec as P

NCLASS = 192
NROT = 36
HIGHEST = lax.Precision.HIGHEST
LAST = (((1,), (1,)), ((), ()))
FIRST = (((0,), (0,)), ((), ()))


def image_moves():
    moves = []
    for x in range(4):
        for h in range(4):
            for y in range(4):
                to_x = (h & 1) * 2 + (y >> 1)
                to_y = (h >> 1) * 2 + (y & 1)
                moves.append(((x * 4 + h) * 4 + y, (to_x * 4 + x) * 4 + to_y))
    return moves


def everywhere(block, axis, size):
    spread = jnp.broadcast_to(block[None], (size,) + block.shape)
    return lax.all_to_all(spread, axis, 0, 0, tiled=True)


def body(images, refs, ctf, ctf_group, class_id, rot_id, class_prior, rot_prior):
    rows, width = images.shape
    ref_rows = refs.shape[0]
    groups = ctf.shape[0]
    img_place = (lax.axis_index("a") * 4 + lax.axis_index("x")) * 2 + lax.axis_index("c")
    ref_place = lax.axis_index("h") * 4 + lax.axis_index("y")

    gathered = lax.all_gather(refs, ("a", "c", "h"), axis=0)

    group_hot = (ctf_group[:, None] == jnp.arange(groups, dtype=jnp.int32)[None, :]).astype(jnp.float32)
    ctf_slab = lax.dynamic_slice_in_dim(ctf, ref_place * width, width, 1)
    ctf_rows = jnp.dot(group_hot, ctf_slab, precision=HIGHEST)
    weighted = (ctf_rows * images.astype(jnp.float32)).astype(jnp.bfloat16)
    moves = image_moves()
    moved = lax.ppermute(weighted, ("x", "h", "y"), moves)
    moved_group = lax.ppermute(ctf_group, ("x", "h", "y"), moves)
    pieces = everywhere(moved, "y", 4)

    ref_slab = lax.dynamic_slice_in_dim(ctf, img_place * width, width, 1)
    ref_float = refs.astype(jnp.float32)
    norm_part = lax.dot_general(ref_slab * ref_slab, ref_float * ref_float, LAST, precision=HIGHEST)
    class_match = class_id[:, None] == jnp.arange(NCLASS, dtype=jnp.int32)[None, :]
    rot_match = rot_id[:, None] == jnp.arange(NROT, dtype=jnp.int32)[None, :]
    priors = jnp.sum(jnp.where(class_match, class_prior[None, :], 0.0), axis=1) + jnp.sum(
        jnp.where(rot_match, rot_prior[None, :], 0.0), axis=1
    )
    facts = jnp.concatenate(
        [norm_part, priors[None], class_id.astype(jnp.float32)[None], jnp.zeros((6, ref_rows), jnp.float32)], 0
    )
    all_facts = lax.all_gather(facts, ("a", "c", "h"), axis=0)
    all_facts = all_facts.reshape(4, 4, 24, ref_rows)
    norms = jnp.sum(all_facts[:, :, :groups], axis=0).transpose(1, 0, 2).reshape(groups, 4 * ref_rows)
    all_priors = all_facts[0, :, groups].reshape(4 * ref_rows)
    all_classes = all_facts[0, :, groups + 1].reshape(4 * ref_rows)

    moved_hot = (moved_group[:, None] == jnp.arange(groups, dtype=jnp.int32)[None, :]).astype(jnp.float32)
    scores = jnp.dot(moved_hot, -0.5 * norms, precision=HIGHEST)
    blocks = gathered.reshape(4, 4 * ref_rows, width)
    for j in range(4):
        scores = scores + lax.dot_general(pieces[j], blocks[j], LAST, preferred_element_type=jnp.float32)

    quarter = rows // 4
    parts = lax.all_to_all(scores.reshape(4, quarter, 4 * ref_rows), "x", 0, 0, tiled=True)
    own = jnp.sum(parts, axis=0) + all_priors[None, :]
    top = jnp.max(own, axis=1)
    class_hot = (all_classes[:, None] == jnp.arange(NCLASS, dtype=jnp.float32)[None, :]).astype(jnp.float32)
    class_part = jnp.dot(jnp.exp(own - top[:, None]), class_hot, precision=HIGHEST)
    payload = jnp.concatenate([class_part, jnp.broadcast_to(top[:, None], (quarter, 64))], axis=1)
    payload = everywhere(payload, "y", 4)
    tops = payload[:, :, NCLASS]
    row_top = jnp.max(tops, axis=0)
    mass = jnp.sum(payload[:, :, :NCLASS] * jnp.exp(tops - row_top[None])[:, :, None], axis=0)
    total = jnp.sum(mass, axis=1)
    evidence = row_top + jnp.log(total)
    posterior = mass / total[:, None]
    payload = jnp.concatenate([posterior, jnp.broadcast_to(evidence[:, None], (quarter, 64))], axis=1)
    swap = [(x * 4 + h, h * 4 + x) for x in range(4) for h in range(4)]
    payload = lax.ppermute(payload, ("x", "h"), swap)
    payload = everywhere(payload, "h", 4).reshape(rows, NCLASS + 64)
    class_post = payload[:, :NCLASS]
    log_evidence = payload[:, NCLASS]

    counts_part = jnp.sum(class_post, axis=0)
    sums_part = lax.dot_general(class_post.astype(jnp.bfloat16), images, FIRST, preferred_element_type=jnp.float32)
    owned = NCLASS // 16
    count_rows = jnp.broadcast_to(jnp.pad(counts_part, (0, width - NCLASS))[None, None], (16, 4, width))
    outgoing = jnp.concatenate([sums_part.reshape(16, owned, width), count_rows], axis=1)
    arrived = jnp.sum(lax.all_to_all(outgoing, ("a", "x", "c"), 0, 0, tiled=True), axis=0)
    counts = arrived[owned, :NCLASS]
    own_counts = lax.dynamic_slice_in_dim(counts, img_place * owned, owned, 0)
    class_avg = arrived[:owned] / (own_counts[:, None] + 1.0)
    occupancy = counts * (NCLASS / (rows * 16))
    return class_avg, occupancy, log_evidence


def solution(mesh):
    split = Mesh(mesh.devices.reshape(2, 4, 2, 4, 4), ("a", "x", "c", "h", "y"))
    img, ref = ("a", "x", "c"), ("h", "y")
    placed = (P(img, ref), P(ref, img), P(), P(img), P(ref), P(ref), P(), P())
    return jax.shard_map(
        body,
        mesh=split,
        in_specs=placed,
        out_specs=(P(img, ref), P(), P(img)),
        check_vma=False,
    )
```

```python
import jax
import jax.numpy as jnp
from jax import lax
from jax.sharding import Mesh, PartitionSpec as P

NCLASS = 192
NROT = 36
HIGHEST = lax.Precision.HIGHEST
LAST = (((1,), (1,)), ((), ()))
FIRST = (((0,), (0,)), ((), ()))
F32 = jnp.float32
BF16 = jnp.bfloat16


def image_moves(part):
    moves = []
    for x in range(4):
        for h in range(4):
            for y in range(4):
                to_x = (h & 1) * 2 + (y >> 1)
                to_y = (h >> 1) * 2 + (y & 1)
                moves.append(((x * 4 + h) * 4 + y, (to_x * 4 + (x ^ part)) * 4 + to_y))
    return moves


def ring(step):
    return [(i, (i + step) % 4) for i in range(4)]


def flip(step):
    return [(i, i ^ step) for i in range(4)]


def swap_core(block):
    return lax.ppermute(block, "c", [(0, 1), (1, 0)])


def at_z(z):
    return (z % 2) * 4 + (z % 8) // 2


def swap_pair(block):
    return lax.ppermute(block, ("a", "h"), [(at_z(z), at_z(z ^ 1)) for z in range(8)])


def swap_cross(block):
    return lax.ppermute(block, ("a", "h"), [(at_z(z), at_z(z - 1 + 2 * (z % 2))) for z in range(8)])


def from_h(block, shift):
    moves = []
    for a in range(2):
        for h in range(4):
            moves.append((a * 4 + (h + (shift if a == 0 else -shift)) % 4, a * 4 + h))
    return lax.ppermute(block, ("a", "h"), moves)


def split3(value):
    first = lax.reduce_precision(value, 8, 7)
    second = lax.reduce_precision(value - first, 8, 7)
    third = value - first - second
    return first.astype(BF16), second.astype(BF16), third.astype(BF16)


def pick(stacked, index):
    return lax.dynamic_index_in_dim(stacked, index, 0, False)


def body(images, refs, ctf, ctf_group, class_id, rot_id, class_prior, rot_prior):
    rows, width = images.shape
    groups = ctf.shape[0]
    quarter = rows // 4
    a, x, c = lax.axis_index("a"), lax.axis_index("x"), lax.axis_index("c")
    h, y = lax.axis_index("h"), lax.axis_index("y")
    img_place = (a * 4 + x) * 2 + c
    ref_place = h * 4 + y

    group_hot = (ctf_group[:, None] == jnp.arange(groups, dtype=jnp.int32)[None, :]).astype(F32)
    ctf_slab = lax.dynamic_slice_in_dim(ctf, ref_place * width, width, 1)
    ctf_rows = jnp.dot(group_hot, ctf_slab, precision=HIGHEST)
    weighted = (ctf_rows * images.astype(F32)).astype(BF16)
    moved = jnp.concatenate(
        [
            lax.ppermute(weighted[p * quarter : (p + 1) * quarter], ("x", "h", "y"), image_moves(p))
            for p in range(4)
        ],
        0,
    )
    right = lax.ppermute(moved, "y", ring(1))
    left = lax.ppermute(moved, "y", ring(-1))
    half = rows // 2
    far = jnp.concatenate(
        [lax.ppermute(right[:half], "y", ring(1)), lax.ppermute(left[half:], "y", ring(-1))], 0
    )
    pieces = jnp.stack([moved, right, far, left])
    own_piece = a * 2 + c
    sides = [pick(pieces, (y - (own_piece ^ q)) % 4) for q in range(4)]

    f1, g1 = swap_pair(refs), swap_cross(refs)
    f2, g2 = swap_pair(g1), swap_cross(f1)
    f3, g3 = swap_pair(g2), swap_cross(f2)
    mid = width // 2
    z4 = jnp.concatenate([swap_cross(f3[:, :mid]), swap_pair(g3[:, mid:])], 1)
    couples = [(refs, f1), (g2, g1), (f2, f3), (z4, g3)]

    class_match = class_id[:, None] == jnp.arange(NCLASS, dtype=jnp.int32)[None, :]
    rot_match = rot_id[:, None] == jnp.arange(NROT, dtype=jnp.int32)[None, :]
    priors = jnp.sum(jnp.where(class_match, class_prior[None, :], 0.0), axis=1) + jnp.sum(
        jnp.where(rot_match, rot_prior[None, :], 0.0), axis=1
    )
    facts = jnp.stack([priors, class_id.astype(F32)])
    all_facts = [facts, from_h(facts, -1), from_h(facts, 1), from_h(facts, 2)]

    near = jnp.stack([ctf_group] + [lax.ppermute(ctf_group, "x", flip(s)) for s in (1, 2, 3)])
    row_groups = jnp.concatenate(
        [pick(near, x ^ h ^ p)[p * quarter : (p + 1) * quarter] for p in range(4)]
    )
    row_hot = (row_groups[:, None] == jnp.arange(groups, dtype=jnp.int32)[None, :]).astype(F32)
    ctf_parts = []
    for q in range(4):
        place = (a ^ (q >> 1)) * 8 + x * 2 + (c ^ (q & 1))
        slab = lax.dynamic_slice_in_dim(ctf, place * width, width, 1)
        ctf_parts.append(jnp.concatenate(split3(slab * slab), 0))

    own = []
    for t in range(4):
        norm, score = 0.0, 0.0
        blocks = [couples[t][0], swap_core(couples[t][0]), couples[t][1], swap_core(couples[t][1])]
        for q in range(4):
            block = blocks[q]
            score += lax.dot_general(sides[q], block, LAST, preferred_element_type=F32)
            square = block.astype(F32) * block.astype(F32)
            high = lax.reduce_precision(square, 8, 7)
            norm += lax.dot_general(ctf_parts[q], high.astype(BF16), LAST, preferred_element_type=F32)
            norm += lax.dot_general(ctf_parts[q], (square - high).astype(BF16), LAST, preferred_element_type=F32)
        norm = norm[:groups] + norm[groups : 2 * groups] + norm[2 * groups :]
        score = score + jnp.dot(row_hot, -0.5 * norm, precision=HIGHEST)
        score = score.reshape(4, quarter, score.shape[1])
        total = pick(score, x ^ h) + all_facts[t][0][None, :]
        for s in (1, 2, 3):
            total = total + lax.ppermute(pick(score, x ^ h ^ s), "x", flip(s))
        own.append(total)

    own = jnp.concatenate(own, 1)
    classes = jnp.concatenate([fact[1] for fact in all_facts])
    top = jnp.max(own, axis=1)
    class_hot = (classes[:, None] == jnp.arange(NCLASS, dtype=F32)[None, :]).astype(F32)
    class_part = jnp.dot(jnp.exp(own - top[:, None]), class_hot, precision=HIGHEST)
    payload = jnp.concatenate([class_part, jnp.broadcast_to(top[:, None], (quarter, 64))], axis=1)
    payload = lax.all_to_all(jnp.broadcast_to(payload[None], (4, quarter, NCLASS + 64)), "y", 0, 0, tiled=True)
    tops = payload[:, :, NCLASS]
    row_top = jnp.max(tops, axis=0)
    mass = jnp.sum(payload[:, :, :NCLASS] * jnp.exp(tops - row_top[None])[:, :, None], axis=0)
    whole = jnp.sum(mass, axis=1)
    evidence = row_top + jnp.log(whole)
    posterior = mass / whole[:, None]

    sent = jnp.concatenate([posterior.astype(BF16)] + [jnp.broadcast_to(e[:, None], (quarter, 16)) for e in split3(evidence)] + [jnp.zeros((quarter, 16), BF16)], 1)
    count_rows = jnp.stack(split3(jnp.sum(posterior, axis=0)))
    sent = jnp.concatenate([sent, jnp.pad(count_rows, ((0, 13), (0, 64)))], 0)
    come = jnp.stack([sent] + [lax.ppermute(sent, "h", flip(s)) for s in (1, 2, 3)])
    come = jnp.stack([pick(come, x ^ h ^ p) for p in range(4)])
    weights = come[:, :quarter, :NCLASS].reshape(rows, NCLASS)
    ev = come[:, :quarter, NCLASS:].astype(F32)
    log_evidence = (ev[:, :, 0] + ev[:, :, 16] + ev[:, :, 32]).reshape(rows)
    counts_part = jnp.sum(come[:, quarter : quarter + 3, :NCLASS].astype(F32), axis=(0, 1))

    sums_part = lax.dot_general(weights, images, FIRST, preferred_element_type=F32)
    owned = NCLASS // 16
    count_rows = jnp.broadcast_to(jnp.pad(counts_part, (0, width - NCLASS))[None, None], (16, 4, width))
    outgoing = jnp.concatenate([sums_part.reshape(16, owned, width), count_rows], axis=1)
    arrived = jnp.sum(lax.all_to_all(outgoing, ("a", "x", "c"), 0, 0, tiled=True), axis=0)
    counts = arrived[owned, :NCLASS]
    own_counts = lax.dynamic_slice_in_dim(counts, img_place * owned, owned, 0)
    class_avg = arrived[:owned] / (own_counts[:, None] + 1.0)
    occupancy = counts * (NCLASS / (rows * 16))
    return class_avg, occupancy, log_evidence


def solution(mesh):
    split = Mesh(mesh.devices.reshape(2, 4, 2, 4, 4), ("a", "x", "c", "h", "y"))
    img, ref = ("a", "x", "c"), ("h", "y")
    placed = (P(img, ref), P(ref, img), P(), P(img), P(ref), P(ref), P(), P())
    return jax.shard_map(
        body,
        mesh=split,
        in_specs=placed,
        out_specs=(P(img, ref), P(), P(img)),
        check_vma=False,
    )
```

```python
import jax
import jax.numpy as jnp
from jax import lax
from jax.experimental import pallas as pl
from jax.experimental.pallas import tpu as pltpu
from jax.sharding import Mesh, PartitionSpec as P

NCLASS = 192
NROT = 36
HIGHEST = lax.Precision.HIGHEST
LAST = (((1,), (1,)), ((), ()))
FIRST = (((0,), (0,)), ((), ()))
F32 = jnp.float32
BF16 = jnp.bfloat16


def image_moves(part):
    moves = []
    for x in range(4):
        for h in range(4):
            for y in range(4):
                to_x = (h & 1) * 2 + (y >> 1)
                to_y = y ^ 3 if h >> 1 else y
                moves.append(((x * 4 + h) * 4 + y, (to_x * 4 + (x ^ part)) * 4 + to_y))
    return moves


def flip(step):
    return [(i, i ^ step) for i in range(4)]


def swap_core(block):
    return lax.ppermute(block, "c", [(0, 1), (1, 0)])


def swap_y(block, step):
    return lax.ppermute(block, "y", flip(step))


def split3(value):
    first = lax.reduce_precision(value, 8, 7)
    second = lax.reduce_precision(value - first, 8, 7)
    third = value - first - second
    return first.astype(BF16), second.astype(BF16), third.astype(BF16)


def pick(stacked, index):
    return lax.dynamic_index_in_dim(stacked, index, 0, False)


def hold(values):
    return lax.optimization_barrier(values)


def product_kernel(order, s0, s1, s2a, s2b, s3, blocks, o0, o1, o2, o3):
    outs = (o0, o1, o2, o3)
    half = s2a.shape[0]
    part = half // 2
    for v in range(4):

        @pl.when(order[0] == v)
        def _():
            use = (v, v ^ 1, v ^ 3, v ^ 2)
            for n in range(2):
                rows = pl.ds(n * half, half)
                images = (s0[rows, :], s1[rows, :], (s2a, s2b)[n][...], s3[rows, :])
                score = None
                for d in range(4):
                    term = lax.dot_general(blocks[0, use[d]], images[d], LAST, preferred_element_type=F32)
                    score = term if score is None else score + term
                outs[2 * n][...] = score[:, :part]
                outs[2 * n + 1][...] = score[:, part:]


def product(order, sides, blocks, first, count):
    cols, width = blocks.shape[2:]
    part = sides[0].shape[0] // 4
    vmem = pl.BlockSpec(memory_space=pltpu.VMEM)
    return pl.pallas_call(
        product_kernel,
        grid=(count,),
        out_shape=[jax.ShapeDtypeStruct((count * cols, part), F32)] * 4,
        in_specs=[pl.BlockSpec(memory_space=pltpu.SMEM)]
        + [vmem] * 5
        + [pl.BlockSpec((1, 4, cols, width), lambda i: (first + i, 0, 0, 0))],
        out_specs=[pl.BlockSpec((cols, part), lambda i: (i, 0))] * 4,
        compiler_params=pltpu.CompilerParams(vmem_limit_bytes=40 * 1024 * 1024),
    )(order, *sides, blocks)


def body(images, refs, ctf, ctf_group, class_id, rot_id, class_prior, rot_prior):
    rows, width = images.shape
    cols = refs.shape[0]
    groups = ctf.shape[0]
    quarter, half, mid = rows // 4, rows // 2, width // 2
    a, x, c = lax.axis_index("a"), lax.axis_index("x"), lax.axis_index("c")
    h, y = lax.axis_index("h"), lax.axis_index("y")
    img_place = (a * 4 + x) * 2 + c
    ref_place = h * 4 + y

    ranges = ((0, cols),)
    gathered = [
        lax.all_gather(refs[low:high], ("h", "a", "c"), axis=0).reshape(4, 4, high - low, width)
        for low, high in ranges
    ]
    group_hot = (ctf_group[:, None] == jnp.arange(groups, dtype=jnp.int32)[None, :]).astype(F32)
    ctf_slab = lax.dynamic_slice_in_dim(ctf, ref_place * width, width, 1)
    ctf_rows = jnp.dot(group_hot, ctf_slab, precision=HIGHEST)
    weighted = (ctf_rows * images.astype(F32)).astype(BF16)
    parts = [weighted[p * quarter : (p + 1) * quarter] for p in range(4)]
    moved = [lax.ppermute(parts[p], ("x", "h", "y"), image_moves(p)) for p in range(4)]

    s0 = jnp.concatenate([lax.select_n(x ^ h ^ s, *moved) for s in range(4)], 0)
    s1, s3 = swap_y(s0, 1), swap_y(s0, 3)
    ref_slab = lax.dynamic_slice_in_dim(ctf, img_place * width, width, 1)
    ref_float = refs.astype(F32)
    norm = lax.dot_general(ref_slab * ref_slab, ref_float * ref_float, LAST, precision=HIGHEST)
    s1, s3, norm = hold((s1, s3, norm))

    s2a, s2b = swap_y(s3[:half], 1), swap_y(s1[half:], 3)
    norm = norm + swap_core(norm)
    norm = norm + lax.ppermute(norm, "x", flip(1))
    norm = norm + lax.ppermute(norm, "x", flip(2))
    s2a, s2b, norm = hold((s2a, s2b, norm))

    norm = norm + lax.ppermute(norm, "a", [(0, 1), (1, 0)])
    class_match = class_id[:, None] == jnp.arange(NCLASS, dtype=jnp.int32)[None, :]
    rot_match = rot_id[:, None] == jnp.arange(NROT, dtype=jnp.int32)[None, :]
    priors = jnp.sum(jnp.where(class_match, class_prior[None, :], 0.0), axis=1) + jnp.sum(
        jnp.where(rot_match, rot_prior[None, :], 0.0), axis=1
    )
    facts = jnp.concatenate([norm, priors[None], class_id.astype(F32)[None], jnp.zeros((6, cols), F32)])
    near = [facts] + [lax.ppermute(facts, "h", flip(s)) for s in (1, 2, 3)]
    all_facts = [lax.select_n(h ^ t, *near) for t in range(4)]
    own_groups = lax.dynamic_slice_in_dim(ctf_group, (x ^ h) * quarter, quarter, 0)
    own_hot = (own_groups[:, None] == jnp.arange(groups, dtype=jnp.int32)[None, :]).astype(F32)
    all_facts, own_hot = hold((all_facts, own_hot))

    turn = (y >> 1) ^ (x & 1)
    order = (2 * turn + ((y & 1) ^ turn)).astype(jnp.int32).reshape(1)
    sides = (s0, s1, s2a, s2b, s3)
    step = len(ranges)
    own, columns = [], []
    for (low, high), blocks in zip(ranges, gathered):
        for t in range(0, 4, step):
            scores = product(order, sides, blocks, t, step)
            total = scores[0]
            for s in (1, 2, 3):
                total = total + lax.ppermute(scores[s], "x", flip(s))
            fact = jnp.concatenate([all_facts[t + n][:, low:high] for n in range(step)], 1)
            offsets = fact[groups][None] - 0.5 * fact[:groups]
            own.append(total + lax.dot_general(offsets, own_hot, (((0,), (1,)), ((), ())), precision=HIGHEST))
            columns.append(fact[groups + 1])

    own = jnp.concatenate(own, 0)
    classes = jnp.concatenate(columns)
    top = jnp.max(own, axis=0)
    class_hot = (classes[:, None] == jnp.arange(NCLASS, dtype=F32)[None, :]).astype(F32)
    class_part = lax.dot_general(class_hot, jnp.exp(own - top[None]), FIRST, precision=HIGHEST)
    payload = jnp.concatenate([class_part, jnp.broadcast_to(top[None], (8, quarter))], axis=0)
    payload = lax.all_to_all(jnp.broadcast_to(payload[None], (4,) + payload.shape), "y", 0, 0, tiled=True)
    tops = payload[:, NCLASS]
    row_top = jnp.max(tops, axis=0)
    mass = jnp.sum(payload[:, :NCLASS] * jnp.exp(tops - row_top[None])[:, None, :], axis=0)
    whole = jnp.sum(mass, axis=0)
    evidence = row_top + jnp.log(whole)
    posterior = mass / whole[None]

    counts_here = jnp.pad(jnp.sum(posterior, axis=1), (0, 2 * quarter - NCLASS))
    sent = jnp.concatenate(
        [
            posterior.astype(BF16),
            jnp.stack(split3(evidence)),
            jnp.concatenate([piece.reshape(2, quarter) for piece in split3(counts_here)]),
            jnp.zeros((7, quarter), BF16),
        ],
        0,
    )
    come = jnp.stack([sent] + [lax.ppermute(sent, "h", flip(s)) for s in (1, 2, 3)])
    come = [pick(come, x ^ h ^ p) for p in range(4)]
    weights = jnp.concatenate([piece[:NCLASS] for piece in come], 1)
    log_evidence = jnp.concatenate([jnp.sum(piece[NCLASS : NCLASS + 3].astype(F32), axis=0) for piece in come])
    counts_part = jnp.zeros((2, quarter), F32)
    for piece in come:
        piece = piece[NCLASS + 3 : NCLASS + 9].astype(F32)
        counts_part = counts_part + (piece[:2] + piece[2:4] + piece[4:])
    counts_part = counts_part.reshape(2 * quarter)

    sums_part = jnp.dot(weights, images, preferred_element_type=F32)
    owned = NCLASS // 16
    count_rows = jnp.broadcast_to(jnp.pad(counts_part, (0, width - 2 * quarter))[None, None], (16, 4, width))
    outgoing = jnp.concatenate([sums_part.reshape(16, owned, width), count_rows], axis=1)
    arrived = jnp.sum(lax.all_to_all(outgoing, ("a", "x", "c"), 0, 0, tiled=True), axis=0)
    counts = arrived[owned, :NCLASS]
    own_counts = lax.dynamic_slice_in_dim(counts, img_place * owned, owned, 0)
    class_avg = arrived[:owned] / (own_counts[:, None] + 1.0)
    occupancy = counts * (NCLASS / (rows * 16))
    return class_avg, occupancy, log_evidence


def solution(mesh):
    split = Mesh(mesh.devices.reshape(2, 4, 2, 4, 4), ("a", "x", "c", "h", "y"))
    img, ref = ("a", "x", "c"), ("h", "y")
    placed = (P(img, ref), P(ref, img), P(), P(img), P(ref), P(ref), P(), P())
    return jax.shard_map(
        body,
        mesh=split,
        in_specs=placed,
        out_specs=(P(img, ref), P(), P(img)),
        check_vma=False,
    )
```

```python
import jax
import jax.numpy as jnp
from jax import lax
from jax.experimental import pallas as pl
from jax.experimental.pallas import tpu as pltpu
from jax.sharding import Mesh, PartitionSpec as P

NCLASS = 192
NROT = 36
HIGHEST = lax.Precision.HIGHEST
LAST = (((1,), (1,)), ((), ()))
FIRST = (((0,), (0,)), ((), ()))
F32 = jnp.float32
BF16 = jnp.bfloat16


def image_moves(part):
    moves = []
    for x in range(4):
        for h in range(4):
            for y in range(4):
                to_x = (h & 1) * 2 + (y >> 1)
                to_y = y ^ 3 if h >> 1 else y
                moves.append(((x * 4 + h) * 4 + y, (to_x * 4 + (x ^ part)) * 4 + to_y))
    return moves


def flip(step):
    return [(i, i ^ step) for i in range(4)]


def swap_core(block):
    return lax.ppermute(block, "c", [(0, 1), (1, 0)])


def swap_y(block, step):
    return lax.ppermute(block, "y", flip(step))


def split3(value):
    first = lax.reduce_precision(value, 8, 7)
    second = lax.reduce_precision(value - first, 8, 7)
    third = value - first - second
    return first.astype(BF16), second.astype(BF16), third.astype(BF16)


def pick(stacked, index):
    return lax.dynamic_index_in_dim(stacked, index, 0, False)


def hold(values):
    return lax.optimization_barrier(values)


def product_kernel(order, s0, s1, s2a, s2b, s3, blocks, o0, o1, o2, o3):
    outs = (o0, o1, o2, o3)
    half = s2a.shape[0]
    part = half // 2
    for v in range(4):

        @pl.when(order[0] == v)
        def _():
            use = (v, v ^ 1, v ^ 3, v ^ 2)
            for n in range(2):
                rows = pl.ds(n * half, half)
                images = (s0[rows, :], s1[rows, :], (s2a, s2b)[n][...], s3[rows, :])
                score = None
                for d in range(4):
                    term = lax.dot_general(blocks[0, use[d]], images[d], LAST, preferred_element_type=F32)
                    score = term if score is None else score + term
                outs[2 * n][...] = score[:, :part]
                outs[2 * n + 1][...] = score[:, part:]


def product(order, sides, blocks):
    count, _, cols, width = blocks.shape
    part = sides[0].shape[0] // 4
    vmem = pl.BlockSpec(memory_space=pltpu.VMEM)
    return pl.pallas_call(
        product_kernel,
        grid=(count,),
        out_shape=[jax.ShapeDtypeStruct((count * cols, part), F32)] * 4,
        in_specs=[pl.BlockSpec(memory_space=pltpu.SMEM)]
        + [vmem] * 5
        + [pl.BlockSpec((1, 4, cols, width), lambda i: (i, 0, 0, 0))],
        out_specs=[pl.BlockSpec((cols, part), lambda i: (i, 0))] * 4,
        compiler_params=pltpu.CompilerParams(vmem_limit_bytes=40 * 1024 * 1024),
    )(order, *sides, blocks)


def body(images, refs, ctf, ctf_group, class_id, rot_id, class_prior, rot_prior):
    rows, width = images.shape
    cols = refs.shape[0]
    groups = ctf.shape[0]
    quarter, half, mid = rows // 4, rows // 2, width // 2
    a, x, c = lax.axis_index("a"), lax.axis_index("x"), lax.axis_index("c")
    h, y = lax.axis_index("h"), lax.axis_index("y")
    img_place = (a * 4 + x) * 2 + c
    ref_place = h * 4 + y

    gathered = lax.all_gather(refs, ("h", "a", "c"), axis=0).reshape(4, 4, cols, width)
    group_hot = (ctf_group[:, None] == jnp.arange(groups, dtype=jnp.int32)[None, :]).astype(F32)
    ctf_slab = lax.dynamic_slice_in_dim(ctf, ref_place * width, width, 1)
    ctf_rows = jnp.dot(group_hot, ctf_slab, precision=HIGHEST)
    weighted = (ctf_rows * images.astype(F32)).astype(BF16)
    parts = [weighted[p * quarter : (p + 1) * quarter] for p in range(4)]
    moved = [lax.ppermute(parts[p], ("x", "h", "y"), image_moves(p)) for p in range(4)]

    ref_slab = lax.dynamic_slice_in_dim(ctf, img_place * width, width, 1)
    ref_float = refs.astype(F32)
    norm = lax.dot_general(ref_slab * ref_slab, ref_float * ref_float, LAST, precision=HIGHEST)
    norm = norm + swap_core(norm)
    moved, norm = hold((moved, norm))

    s0 = jnp.concatenate([lax.select_n(x ^ h ^ s, *moved) for s in range(4)], 0)
    s1, s3 = swap_y(s0, 1), swap_y(s0, 3)
    norm = norm + lax.ppermute(norm, "x", flip(1))
    norm = norm + lax.ppermute(norm, "x", flip(2))
    s1, s3, norm = hold((s1, s3, norm))
    s2a, s2b = swap_y(s3[:half], 1), swap_y(s1[half:], 3)

    class_match = class_id[:, None] == jnp.arange(NCLASS, dtype=jnp.int32)[None, :]
    rot_match = rot_id[:, None] == jnp.arange(NROT, dtype=jnp.int32)[None, :]
    priors = jnp.sum(jnp.where(class_match, class_prior[None, :], 0.0), axis=1) + jnp.sum(
        jnp.where(rot_match, rot_prior[None, :], 0.0), axis=1
    )
    norm = norm + lax.ppermute(norm, "a", [(0, 1), (1, 0)])
    facts = jnp.concatenate([norm, priors[None], class_id.astype(F32)[None], jnp.zeros((6, cols), F32)])
    near = [facts] + [lax.ppermute(facts, "h", flip(s)) for s in (1, 2, 3)]
    facts = jnp.concatenate([lax.select_n(h ^ t, *near) for t in range(4)], 1)
    own_groups = lax.dynamic_slice_in_dim(ctf_group, (x ^ h) * quarter, quarter, 0)
    own_hot = (own_groups[:, None] == jnp.arange(groups, dtype=jnp.int32)[None, :]).astype(F32)
    offsets = facts[groups][None] - 0.5 * facts[:groups]
    offsets = lax.dot_general(offsets, own_hot, (((0,), (1,)), ((), ())), precision=HIGHEST)
    class_hot = (facts[groups + 1][:, None] == jnp.arange(NCLASS, dtype=F32)[None, :]).astype(BF16)
    s2a, s2b, offsets, class_hot = hold((s2a, s2b, offsets, class_hot))

    turn = (y >> 1) ^ (x & 1)
    order = (2 * turn + ((y & 1) ^ turn)).astype(jnp.int32).reshape(1)
    scores = product(order, (s0, s1, s2a, s2b, s3), gathered)

    def part(s, n):
        return scores[s][n * cols : (n + 1) * cols]

    halves = [
        (lax.ppermute(part(2, n), "x", flip(3)), lax.ppermute(part(2, n + 1), "x", flip(1))) for n in (0, 2)
    ]
    own = []
    for n, (to3, to1) in zip((0, 2), halves):
        part1 = jnp.concatenate([part(1, n) + to3, part(1, n + 1)], 0)
        part3 = jnp.concatenate([part(3, n), part(3, n + 1) + to1], 0)
        here = scores[0][n * cols : (n + 2) * cols] + offsets[n * cols : (n + 2) * cols]
        own.append(here + lax.ppermute(part1, "x", flip(1)) + lax.ppermute(part3, "x", flip(3)))

    own = jnp.concatenate(own, 0)
    top = jnp.max(own, axis=0)
    terms = jnp.concatenate(split3(jnp.exp(own - top[None])), 1)
    class_part = lax.dot_general(class_hot, terms, FIRST, preferred_element_type=F32)
    class_part = class_part[:, :quarter] + class_part[:, quarter : 2 * quarter] + class_part[:, 2 * quarter :]
    payload = jnp.concatenate([class_part, jnp.broadcast_to(top[None], (8, quarter))], axis=0)
    payload = lax.all_to_all(jnp.broadcast_to(payload[None], (4,) + payload.shape), "y", 0, 0, tiled=True)
    tops = payload[:, NCLASS]
    row_top = jnp.max(tops, axis=0)
    mass = jnp.sum(payload[:, :NCLASS] * jnp.exp(tops - row_top[None])[:, None, :], axis=0)
    whole = jnp.sum(mass, axis=0)
    evidence = row_top + jnp.log(whole)
    posterior = mass / whole[None]

    counts_here = jnp.pad(jnp.sum(posterior, axis=1), (0, 2 * quarter - NCLASS))
    sent = jnp.concatenate(
        [
            posterior.astype(BF16),
            jnp.stack(split3(evidence)),
            jnp.concatenate([piece.reshape(2, quarter) for piece in split3(counts_here)]),
            jnp.zeros((7, quarter), BF16),
        ],
        0,
    )
    come = jnp.stack([sent] + [lax.ppermute(sent, "h", flip(s)) for s in (1, 2, 3)])
    come = [pick(come, x ^ h ^ p) for p in range(4)]
    weights = jnp.concatenate([piece[:NCLASS] for piece in come], 1)
    log_evidence = jnp.concatenate([jnp.sum(piece[NCLASS : NCLASS + 3].astype(F32), axis=0) for piece in come])
    counts_part = jnp.zeros((2, quarter), F32)
    for piece in come:
        piece = piece[NCLASS + 3 : NCLASS + 9].astype(F32)
        counts_part = counts_part + (piece[:2] + piece[2:4] + piece[4:])
    counts_part = counts_part.reshape(2 * quarter)

    sums_part = jnp.dot(weights, images, preferred_element_type=F32)
    owned = NCLASS // 16
    count_rows = jnp.pad(jnp.stack(split3(counts_part)), ((0, 1), (0, width - 2 * quarter)))
    outgoing = jnp.concatenate(
        [sums_part.astype(BF16).reshape(16, owned, width), jnp.broadcast_to(count_rows[None], (16, 4, width))], axis=1
    )
    arrived = lax.all_to_all(outgoing, ("a", "x", "c"), 0, 0, tiled=True).astype(F32)
    arrived = jnp.sum(arrived, axis=0)
    counts = jnp.sum(arrived[owned : owned + 3, :NCLASS], axis=0)
    own_counts = lax.dynamic_slice_in_dim(counts, img_place * owned, owned, 0)
    class_avg = arrived[:owned] / (own_counts[:, None] + 1.0)
    occupancy = counts * (NCLASS / (rows * 16))
    return class_avg, occupancy, log_evidence


def solution(mesh):
    split = Mesh(mesh.devices.reshape(2, 4, 2, 4, 4), ("a", "x", "c", "h", "y"))
    img, ref = ("a", "x", "c"), ("h", "y")
    placed = (P(img, ref), P(ref, img), P(), P(img), P(ref), P(ref), P(), P())
    return jax.shard_map(
        body,
        mesh=split,
        in_specs=placed,
        out_specs=(P(img, ref), P(), P(img)),
        check_vma=False,
    )
```

```python
import jax
import jax.numpy as jnp
from jax import lax
from jax.experimental import pallas as pl
from jax.experimental.pallas import tpu as pltpu
from jax.sharding import Mesh, PartitionSpec as P

NCLASS = 192
NROT = 36
HIGHEST = lax.Precision.HIGHEST
LAST = (((1,), (1,)), ((), ()))
FIRST = (((0,), (0,)), ((), ()))
F32 = jnp.float32
BF16 = jnp.bfloat16


def image_moves(part):
    moves = []
    for x in range(4):
        for h in range(4):
            for y in range(4):
                to_x = (h & 1) * 2 + (y >> 1)
                to_y = y ^ 3 if h >> 1 else y
                moves.append(((x * 4 + h) * 4 + y, (to_x * 4 + (x ^ part)) * 4 + to_y))
    return moves


def flip(step):
    return [(i, i ^ step) for i in range(4)]


def swap_core(block):
    return lax.ppermute(block, "c", [(0, 1), (1, 0)])


def swap_y(block, step):
    return lax.ppermute(block, "y", flip(step))


def split3(value):
    first = lax.reduce_precision(value, 8, 7)
    second = lax.reduce_precision(value - first, 8, 7)
    third = value - first - second
    return first.astype(BF16), second.astype(BF16), third.astype(BF16)


def pick(stacked, index):
    return lax.dynamic_index_in_dim(stacked, index, 0, False)


def hold(values):
    return lax.optimization_barrier(values)


def product_kernel(order, s0, s1, s2a, s2b, s3, blocks, o0, o1, o2, o3):
    outs = (o0, o1, o2, o3)
    half = s2a.shape[0]
    part = half // 2
    for v in range(4):

        @pl.when(order[0] == v)
        def _():
            use = (v, v ^ 1, v ^ 3, v ^ 2)
            for n in range(2):
                rows = pl.ds(n * half, half)
                images = (s0[rows, :], s1[rows, :], (s2a, s2b)[n][...], s3[rows, :])
                score = None
                for d in range(4):
                    term = lax.dot_general(blocks[0, use[d]], images[d], LAST, preferred_element_type=F32)
                    score = term if score is None else score + term
                outs[2 * n][...] = score[:, :part]
                outs[2 * n + 1][...] = score[:, part:]


def product(order, sides, blocks):
    count, _, cols, width = blocks.shape
    part = sides[0].shape[0] // 4
    vmem = pl.BlockSpec(memory_space=pltpu.VMEM)
    return pl.pallas_call(
        product_kernel,
        grid=(count,),
        out_shape=[jax.ShapeDtypeStruct((count * cols, part), F32)] * 4,
        in_specs=[pl.BlockSpec(memory_space=pltpu.SMEM)]
        + [vmem] * 5
        + [pl.BlockSpec((1, 4, cols, width), lambda i: (i, 0, 0, 0))],
        out_specs=[pl.BlockSpec((cols, part), lambda i: (i, 0))] * 4,
        compiler_params=pltpu.CompilerParams(vmem_limit_bytes=40 * 1024 * 1024),
    )(order, *sides, blocks)


def body(images, refs, ctf, ctf_group, class_id, rot_id, class_prior, rot_prior):
    rows, width = images.shape
    cols = refs.shape[0]
    groups = ctf.shape[0]
    quarter, half, mid = rows // 4, rows // 2, width // 2
    a, x, c = lax.axis_index("a"), lax.axis_index("x"), lax.axis_index("c")
    h, y = lax.axis_index("h"), lax.axis_index("y")
    img_place = (a * 4 + x) * 2 + c
    ref_place = h * 4 + y

    gathered = lax.all_gather(refs, ("h", "a", "c"), axis=0).reshape(4, 4, cols, width)
    group_hot = (ctf_group[:, None] == jnp.arange(groups, dtype=jnp.int32)[None, :]).astype(F32)
    ctf_slab = lax.dynamic_slice_in_dim(ctf, ref_place * width, width, 1)
    ctf_rows = jnp.dot(group_hot, ctf_slab, precision=HIGHEST)
    weighted = (ctf_rows * images.astype(F32)).astype(BF16)
    parts = [weighted[p * quarter : (p + 1) * quarter] for p in range(4)]
    moved = [lax.ppermute(parts[p], ("x", "h", "y"), image_moves(p)) for p in range(4)]

    ref_slab = lax.dynamic_slice_in_dim(ctf, img_place * width, width, 1)
    ref_float = refs.astype(F32)
    norm = lax.dot_general(ref_slab * ref_slab, ref_float * ref_float, LAST, precision=HIGHEST)
    norm = norm + swap_core(norm)
    moved, norm = hold((moved, norm))

    s0 = jnp.concatenate([lax.select_n(x ^ h ^ s, *moved) for s in range(4)], 0)
    s1, s3 = swap_y(s0, 1), swap_y(s0, 3)
    norm = norm + lax.ppermute(norm, "x", flip(1))
    norm = norm + lax.ppermute(norm, "x", flip(2))
    s1, s3, norm = hold((s1, s3, norm))
    s2a, s2b = swap_y(s3[:half], 1), swap_y(s1[half:], 3)

    class_match = class_id[:, None] == jnp.arange(NCLASS, dtype=jnp.int32)[None, :]
    rot_match = rot_id[:, None] == jnp.arange(NROT, dtype=jnp.int32)[None, :]
    priors = jnp.sum(jnp.where(class_match, class_prior[None, :], 0.0), axis=1) + jnp.sum(
        jnp.where(rot_match, rot_prior[None, :], 0.0), axis=1
    )
    norm = norm + lax.ppermute(norm, "a", [(0, 1), (1, 0)])
    facts = jnp.concatenate([norm, priors[None], class_id.astype(F32)[None], jnp.zeros((6, cols), F32)])
    near = [facts] + [lax.ppermute(facts, "h", flip(s)) for s in (1, 2, 3)]
    facts = jnp.concatenate([lax.select_n(h ^ t, *near) for t in range(4)], 1)
    own_groups = lax.dynamic_slice_in_dim(ctf_group, (x ^ h) * quarter, quarter, 0)
    own_hot = (own_groups[:, None] == jnp.arange(groups, dtype=jnp.int32)[None, :]).astype(F32)
    offsets = facts[groups][None] - 0.5 * facts[:groups]
    offsets = lax.dot_general(offsets, own_hot, (((0,), (1,)), ((), ())), precision=HIGHEST)
    class_hot = (facts[groups + 1][:, None] == jnp.arange(NCLASS, dtype=F32)[None, :]).astype(BF16)
    s2a, s2b, offsets, class_hot = hold((s2a, s2b, offsets, class_hot))

    turn = (y >> 1) ^ (x & 1)
    order = (2 * turn + ((y & 1) ^ turn)).astype(jnp.int32).reshape(1)
    own = []
    products = product(order, (s0, s1, s2a, s2b, s3), gathered)
    for n in (0, 2):
        scores = [piece[n * cols : (n + 2) * cols] for piece in products]
        to3 = lax.ppermute(scores[2][:cols], "x", flip(3))
        to1 = lax.ppermute(scores[2][cols:], "x", flip(1))
        part1 = jnp.concatenate([scores[1][:cols] + to3, scores[1][cols:]], 0)
        part3 = jnp.concatenate([scores[3][:cols], scores[3][cols:] + to1], 0)
        here = scores[0] + offsets[n * cols : (n + 2) * cols]
        own.append(here + lax.ppermute(part1, "x", flip(1)) + lax.ppermute(part3, "x", flip(3)))

    own = jnp.concatenate(own, 0)
    top = jnp.max(own, axis=0)
    terms = jnp.concatenate(split3(jnp.exp(own - top[None])), 1)
    class_part = lax.dot_general(class_hot, terms, FIRST, preferred_element_type=F32)
    class_part = class_part[:, :quarter] + class_part[:, quarter : 2 * quarter] + class_part[:, 2 * quarter :]
    payload = jnp.concatenate([class_part, jnp.broadcast_to(top[None], (8, quarter))], axis=0)
    payload = lax.all_to_all(jnp.broadcast_to(payload[None], (4,) + payload.shape), "y", 0, 0, tiled=True)
    tops = payload[:, NCLASS]
    row_top = jnp.max(tops, axis=0)
    mass = jnp.sum(payload[:, :NCLASS] * jnp.exp(tops - row_top[None])[:, None, :], axis=0)
    whole = jnp.sum(mass, axis=0)
    evidence = row_top + jnp.log(whole)
    posterior = mass / whole[None]

    counts_here = jnp.pad(jnp.sum(posterior, axis=1), (0, 2 * quarter - NCLASS))
    sent = jnp.concatenate(
        [
            posterior.astype(BF16),
            jnp.stack(split3(evidence)),
            jnp.concatenate([piece.reshape(2, quarter) for piece in split3(counts_here)]),
            jnp.zeros((7, quarter), BF16),
        ],
        0,
    )
    come = jnp.stack([sent] + [lax.ppermute(sent, "h", flip(s)) for s in (1, 2, 3)])
    come = [pick(come, x ^ h ^ p) for p in range(4)]
    weights = jnp.concatenate([piece[:NCLASS] for piece in come], 1)
    log_evidence = jnp.concatenate([jnp.sum(piece[NCLASS : NCLASS + 3].astype(F32), axis=0) for piece in come])
    counts_part = jnp.zeros((2, quarter), F32)
    for piece in come:
        piece = piece[NCLASS + 3 : NCLASS + 9].astype(F32)
        counts_part = counts_part + (piece[:2] + piece[2:4] + piece[4:])
    counts_part = counts_part.reshape(2 * quarter)

    owned = NCLASS // 16
    weights = weights.reshape(8, 2, owned, rows)
    count_row = jnp.pad(counts_part, (0, width - 2 * quarter))

    def sums_of(core):
        kept = jnp.pad(lax.dynamic_index_in_dim(weights, core, 1, False), ((0, 0), (0, 4), (0, 0)))
        sums = jnp.dot(kept.reshape(8 * (owned + 4), rows), images, preferred_element_type=F32)
        sums = sums.reshape(8, owned + 4, width)
        place = lax.broadcasted_iota(jnp.int32, sums.shape, 1)
        return jnp.where(place == owned, count_row[None, None], sums)

    outgoing = sums_of(c) + swap_core(sums_of(1 - c))
    arrived = jnp.sum(lax.all_to_all(outgoing, ("a", "x"), 0, 0, tiled=True), axis=0)
    counts = arrived[owned, :NCLASS]
    own_counts = lax.dynamic_slice_in_dim(counts, img_place * owned, owned, 0)
    class_avg = arrived[:owned] / (own_counts[:, None] + 1.0)
    occupancy = counts * (NCLASS / (rows * 16))
    return class_avg, occupancy, log_evidence


def solution(mesh):
    split = Mesh(mesh.devices.reshape(2, 4, 2, 4, 4), ("a", "x", "c", "h", "y"))
    img, ref = ("a", "x", "c"), ("h", "y")
    placed = (P(img, ref), P(ref, img), P(), P(img), P(ref), P(ref), P(), P())
    return jax.shard_map(
        body,
        mesh=split,
        in_specs=placed,
        out_specs=(P(img, ref), P(), P(img)),
        check_vma=False,
    )
```

```python
import jax
import jax.numpy as jnp
from jax import lax
from jax.experimental import pallas as pl
from jax.experimental.pallas import tpu as pltpu
from jax.sharding import Mesh, PartitionSpec as P

NCLASS = 192
NROT = 36
HIGHEST = lax.Precision.HIGHEST
LAST = (((1,), (1,)), ((), ()))
FIRST = (((0,), (0,)), ((), ()))
F32 = jnp.float32
BF16 = jnp.bfloat16


def image_moves(part):
    moves = []
    for x in range(4):
        for h in range(4):
            for y in range(4):
                to_x = (h & 1) * 2 + (y >> 1)
                to_y = y ^ 3 if h >> 1 else y
                moves.append(((x * 4 + h) * 4 + y, (to_x * 4 + (x ^ part)) * 4 + to_y))
    return moves


def flip(step):
    return [(i, i ^ step) for i in range(4)]


def swap_core(block):
    return lax.ppermute(block, "c", [(0, 1), (1, 0)])


def swap_y(block, step):
    return lax.ppermute(block, "y", flip(step))


def split3(value):
    first = lax.reduce_precision(value, 8, 7)
    second = lax.reduce_precision(value - first, 8, 7)
    third = value - first - second
    return first.astype(BF16), second.astype(BF16), third.astype(BF16)


def pick(stacked, index):
    return lax.dynamic_index_in_dim(stacked, index, 0, False)


def hold(values):
    return lax.optimization_barrier(values)


def product_kernel(order, s0, s1, s2a, s2b, s3, blocks, o0, o1, o2, o3):
    outs = (o0, o1, o2, o3)
    half = s2a.shape[0]
    part = half // 2
    for v in range(4):

        @pl.when(order[0] == v)
        def _():
            use = (v, v ^ 1, v ^ 3, v ^ 2)
            for n in range(2):
                rows = pl.ds(n * half, half)
                images = (s0[rows, :], s1[rows, :], (s2a, s2b)[n][...], s3[rows, :])
                score = None
                for d in range(4):
                    term = lax.dot_general(blocks[0, use[d]], images[d], LAST, preferred_element_type=F32)
                    score = term if score is None else score + term
                outs[2 * n][...] = score[:, :part]
                outs[2 * n + 1][...] = score[:, part:]


def product(order, sides, blocks, first, count):
    cols, width = blocks.shape[2:]
    part = sides[0].shape[0] // 4
    vmem = pl.BlockSpec(memory_space=pltpu.VMEM)
    return pl.pallas_call(
        product_kernel,
        grid=(count,),
        out_shape=[jax.ShapeDtypeStruct((count * cols, part), F32)] * 4,
        in_specs=[pl.BlockSpec(memory_space=pltpu.SMEM)]
        + [vmem] * 5
        + [pl.BlockSpec((1, 4, cols, width), lambda i: (first + i, 0, 0, 0))],
        out_specs=[pl.BlockSpec((cols, part), lambda i: (i, 0))] * 4,
        compiler_params=pltpu.CompilerParams(vmem_limit_bytes=40 * 1024 * 1024),
    )(order, *sides, blocks)


def body(images, refs, ctf, ctf_group, class_id, rot_id, class_prior, rot_prior):
    rows, width = images.shape
    cols = refs.shape[0]
    groups = ctf.shape[0]
    quarter, half, mid = rows // 4, rows // 2, width // 2
    a, x, c = lax.axis_index("a"), lax.axis_index("x"), lax.axis_index("c")
    h, y = lax.axis_index("h"), lax.axis_index("y")
    img_place = (a * 4 + x) * 2 + c
    ref_place = h * 4 + y

    gathered = lax.all_gather(refs, ("h", "a", "c"), axis=0).reshape(4, 4, cols, width)
    group_hot = (ctf_group[:, None] == jnp.arange(groups, dtype=jnp.int32)[None, :]).astype(F32)
    ctf_slab = lax.dynamic_slice_in_dim(ctf, ref_place * width, width, 1)
    ctf_rows = jnp.dot(group_hot, ctf_slab, precision=HIGHEST)
    weighted = (ctf_rows * images.astype(F32)).astype(BF16)
    parts = [weighted[p * quarter : (p + 1) * quarter] for p in range(4)]
    moved = [lax.ppermute(parts[p], ("x", "h", "y"), image_moves(p)) for p in range(4)]

    ref_slab = lax.dynamic_slice_in_dim(ctf, img_place * width, width, 1)
    ref_float = refs.astype(F32)
    norm = lax.dot_general(ref_slab * ref_slab, ref_float * ref_float, LAST, precision=HIGHEST)
    norm = norm + swap_core(norm)
    moved, norm = hold((moved, norm))

    s0 = jnp.concatenate([lax.select_n(x ^ h ^ s, *moved) for s in range(4)], 0)
    s1, s3 = swap_y(s0, 1), swap_y(s0, 3)
    norm = norm + lax.ppermute(norm, "x", flip(1))
    norm = norm + lax.ppermute(norm, "x", flip(2))
    s1, s3, norm = hold((s1, s3, norm))
    s2a, s2b = swap_y(s3[:half], 1), swap_y(s1[half:], 3)

    class_match = class_id[:, None] == jnp.arange(NCLASS, dtype=jnp.int32)[None, :]
    rot_match = rot_id[:, None] == jnp.arange(NROT, dtype=jnp.int32)[None, :]
    priors = jnp.sum(jnp.where(class_match, class_prior[None, :], 0.0), axis=1) + jnp.sum(
        jnp.where(rot_match, rot_prior[None, :], 0.0), axis=1
    )
    norm = norm + lax.ppermute(norm, "a", [(0, 1), (1, 0)])
    facts = jnp.concatenate([norm, priors[None], class_id.astype(F32)[None], jnp.zeros((6, cols), F32)])
    near = [facts] + [lax.ppermute(facts, "h", flip(s)) for s in (1, 2, 3)]
    facts = jnp.concatenate([lax.select_n(h ^ t, *near) for t in range(4)], 1)
    own_groups = lax.dynamic_slice_in_dim(ctf_group, (x ^ h) * quarter, quarter, 0)
    own_hot = (own_groups[:, None] == jnp.arange(groups, dtype=jnp.int32)[None, :]).astype(F32)
    offsets = facts[groups][None] - 0.5 * facts[:groups]
    offsets = lax.dot_general(offsets, own_hot, (((0,), (1,)), ((), ())), precision=HIGHEST)
    class_hot = (facts[groups + 1][:, None] == jnp.arange(NCLASS, dtype=F32)[None, :]).astype(BF16)
    s2a, s2b, offsets, class_hot = hold((s2a, s2b, offsets, class_hot))

    turn = (y >> 1) ^ (x & 1)
    order = (2 * turn + ((y & 1) ^ turn)).astype(jnp.int32).reshape(1)
    own = []
    for n in (0, 2):
        scores = product(order, (s0, s1, s2a, s2b, s3), gathered, n, 2)
        to3 = lax.ppermute(scores[2][:cols], "x", flip(3))
        to1 = lax.ppermute(scores[2][cols:], "x", flip(1))
        part1 = jnp.concatenate([scores[1][:cols] + to3, scores[1][cols:]], 0)
        part3 = jnp.concatenate([scores[3][:cols], scores[3][cols:] + to1], 0)
        here = scores[0] + offsets[n * cols : (n + 2) * cols]
        own.append(here + lax.ppermute(part1, "x", flip(1)) + lax.ppermute(part3, "x", flip(3)))

    own = jnp.concatenate(own, 0)
    top = jnp.max(own, axis=0)
    terms = jnp.concatenate(split3(jnp.exp(own - top[None])), 1)
    class_part = lax.dot_general(class_hot, terms, FIRST, preferred_element_type=F32)
    class_part = class_part[:, :quarter] + class_part[:, quarter : 2 * quarter] + class_part[:, 2 * quarter :]
    payload = jnp.concatenate([class_part, jnp.broadcast_to(top[None], (8, quarter))], axis=0)
    near = [payload] + [swap_y(payload, step) for step in (1, 2, 3)]
    payload = jnp.stack([lax.select_n(y ^ place, *near) for place in range(4)])
    tops = payload[:, NCLASS]
    row_top = jnp.max(tops, axis=0)
    mass = jnp.sum(payload[:, :NCLASS] * jnp.exp(tops - row_top[None])[:, None, :], axis=0)
    whole = jnp.sum(mass, axis=0)
    evidence = row_top + jnp.log(whole)
    posterior = mass / whole[None]

    counts_here = jnp.pad(jnp.sum(posterior, axis=1), (0, 2 * quarter - NCLASS))
    sent = jnp.concatenate(
        [
            posterior.astype(BF16),
            jnp.stack(split3(evidence)),
            jnp.concatenate([piece.reshape(2, quarter) for piece in split3(counts_here)]),
            jnp.zeros((7, quarter), BF16),
        ],
        0,
    )
    come = jnp.stack([sent] + [lax.ppermute(sent, "h", flip(s)) for s in (1, 2, 3)])
    come = [pick(come, x ^ h ^ p) for p in range(4)]
    weights = jnp.concatenate([piece[:NCLASS] for piece in come], 1)
    log_evidence = jnp.concatenate([jnp.sum(piece[NCLASS : NCLASS + 3].astype(F32), axis=0) for piece in come])
    counts_part = jnp.zeros((2, quarter), F32)
    for piece in come:
        piece = piece[NCLASS + 3 : NCLASS + 9].astype(F32)
        counts_part = counts_part + (piece[:2] + piece[2:4] + piece[4:])
    counts_part = counts_part.reshape(2 * quarter)

    owned = NCLASS // 16
    weights = weights.reshape(8, 2, owned, rows)
    count_row = jnp.pad(counts_part, (0, width - 2 * quarter))

    def sums_of(core):
        kept = jnp.pad(lax.dynamic_index_in_dim(weights, core, 1, False), ((0, 0), (0, 4), (0, 0)))
        sums = jnp.dot(kept.reshape(8 * (owned + 4), rows), images, preferred_element_type=F32)
        sums = sums.reshape(8, owned + 4, width)
        place = lax.broadcasted_iota(jnp.int32, sums.shape, 1)
        return jnp.where(place == owned, count_row[None, None], sums)

    outgoing = sums_of(c) + swap_core(sums_of(1 - c))
    arrived = jnp.sum(lax.all_to_all(outgoing, ("a", "x"), 0, 0, tiled=True), axis=0)
    counts = arrived[owned, :NCLASS]
    own_counts = lax.dynamic_slice_in_dim(counts, img_place * owned, owned, 0)
    class_avg = arrived[:owned] / (own_counts[:, None] + 1.0)
    occupancy = counts * (NCLASS / (rows * 16))
    return class_avg, occupancy, log_evidence


def solution(mesh):
    split = Mesh(mesh.devices.reshape(2, 4, 2, 4, 4), ("a", "x", "c", "h", "y"))
    img, ref = ("a", "x", "c"), ("h", "y")
    placed = (P(img, ref), P(ref, img), P(), P(img), P(ref), P(ref), P(), P())
    return jax.shard_map(
        body,
        mesh=split,
        in_specs=placed,
        out_specs=(P(img, ref), P(), P(img)),
        check_vma=False,
    )
```

```python
import jax
import jax.numpy as jnp
from jax import lax
from jax.experimental import pallas as pl
from jax.experimental.pallas import tpu as pltpu
from jax.sharding import Mesh, PartitionSpec as P

NCLASS = 192
NROT = 36
HIGHEST = lax.Precision.HIGHEST
LAST = (((1,), (1,)), ((), ()))
FIRST = (((0,), (0,)), ((), ()))
F32 = jnp.float32
BF16 = jnp.bfloat16


def image_moves(part):
    moves = []
    for x in range(4):
        for h in range(4):
            for y in range(4):
                to_x = (h & 1) * 2 + (y >> 1)
                to_y = y ^ 3 if h >> 1 else y
                moves.append(((x * 4 + h) * 4 + y, (to_x * 4 + (x ^ part)) * 4 + to_y))
    return moves


def flip(step):
    return [(i, i ^ step) for i in range(4)]


def swap_core(block):
    return lax.ppermute(block, "c", [(0, 1), (1, 0)])


def swap_y(block, step):
    return lax.ppermute(block, "y", flip(step))


def split3(value):
    first = lax.reduce_precision(value, 8, 7)
    second = lax.reduce_precision(value - first, 8, 7)
    third = value - first - second
    return first.astype(BF16), second.astype(BF16), third.astype(BF16)


def pick(stacked, index):
    return lax.dynamic_index_in_dim(stacked, index, 0, False)


def hold(values):
    return lax.optimization_barrier(values)


def product_kernel(order, s0, s1, s2a, s2b, s3, blocks, o0, o1, o2, o3):
    outs = (o0, o1, o2, o3)
    half = s2a.shape[0]
    part = half // 2
    for v in range(4):

        @pl.when(order[0] == v)
        def _():
            use = (v, v ^ 1, v ^ 3, v ^ 2)
            for n in range(2):
                rows = pl.ds(n * half, half)
                images = (s0[rows, :], s1[rows, :], (s2a, s2b)[n][...], s3[rows, :])
                score = None
                for d in range(4):
                    term = lax.dot_general(blocks[0, use[d]], images[d], LAST, preferred_element_type=F32)
                    score = term if score is None else score + term
                outs[2 * n][...] = score[:, :part]
                outs[2 * n + 1][...] = score[:, part:]


def product(order, sides, blocks, first, count):
    cols, width = blocks.shape[2:]
    part = sides[0].shape[0] // 4
    vmem = pl.BlockSpec(memory_space=pltpu.VMEM)
    return pl.pallas_call(
        product_kernel,
        grid=(count,),
        out_shape=[jax.ShapeDtypeStruct((count * cols, part), F32)] * 4,
        in_specs=[pl.BlockSpec(memory_space=pltpu.SMEM)]
        + [vmem] * 5
        + [pl.BlockSpec((1, 4, cols, width), lambda i: (first + i, 0, 0, 0))],
        out_specs=[pl.BlockSpec((cols, part), lambda i: (i, 0))] * 4,
        compiler_params=pltpu.CompilerParams(vmem_limit_bytes=40 * 1024 * 1024),
    )(order, *sides, blocks)


def body(images, refs, ctf, ctf_group, class_id, rot_id, class_prior, rot_prior):
    rows, width = images.shape
    cols = refs.shape[0]
    groups = ctf.shape[0]
    quarter, half, mid = rows // 4, rows // 2, width // 2
    a, x, c = lax.axis_index("a"), lax.axis_index("x"), lax.axis_index("c")
    h, y = lax.axis_index("h"), lax.axis_index("y")
    img_place = (a * 4 + x) * 2 + c
    ref_place = h * 4 + y

    gathered = lax.all_gather(refs, ("h", "a", "c"), axis=0).reshape(4, 4, cols, width)
    group_hot = (ctf_group[:, None] == jnp.arange(groups, dtype=jnp.int32)[None, :]).astype(F32)
    ctf_slab = lax.dynamic_slice_in_dim(ctf, ref_place * width, width, 1)
    ctf_rows = jnp.dot(group_hot, ctf_slab, precision=HIGHEST)
    weighted = (ctf_rows * images.astype(F32)).astype(BF16)
    parts = [weighted[p * quarter : (p + 1) * quarter] for p in range(4)]
    moved = [lax.ppermute(parts[p], ("x", "h", "y"), image_moves(p)) for p in range(4)]

    ref_slab = lax.dynamic_slice_in_dim(ctf, img_place * width, width, 1)
    ref_float = refs.astype(F32)
    norm = lax.dot_general(ref_slab * ref_slab, ref_float * ref_float, LAST, precision=HIGHEST)
    norm = norm + swap_core(norm)
    moved, norm = hold((moved, norm))

    s0 = jnp.concatenate([lax.select_n(x ^ h ^ s, *moved) for s in range(4)], 0)
    s1, s3 = swap_y(s0, 1), swap_y(s0, 3)
    norm = norm + lax.ppermute(norm, "x", flip(1))
    norm = norm + lax.ppermute(norm, "x", flip(2))
    s1, s3, norm = hold((s1, s3, norm))
    s2a, s2b = swap_y(s3[:half], 1), swap_y(s1[half:], 3)

    class_match = class_id[:, None] == jnp.arange(NCLASS, dtype=jnp.int32)[None, :]
    rot_match = rot_id[:, None] == jnp.arange(NROT, dtype=jnp.int32)[None, :]
    priors = jnp.sum(jnp.where(class_match, class_prior[None, :], 0.0), axis=1) + jnp.sum(
        jnp.where(rot_match, rot_prior[None, :], 0.0), axis=1
    )
    norm = norm + lax.ppermute(norm, "a", [(0, 1), (1, 0)])
    facts = jnp.concatenate([norm, priors[None], class_id.astype(F32)[None], jnp.zeros((6, cols), F32)])
    near = [facts] + [lax.ppermute(facts, "h", flip(s)) for s in (1, 2, 3)]
    facts = jnp.concatenate([lax.select_n(h ^ t, *near) for t in range(4)], 1)
    own_groups = lax.dynamic_slice_in_dim(ctf_group, (x ^ h) * quarter, quarter, 0)
    own_hot = (own_groups[:, None] == jnp.arange(groups, dtype=jnp.int32)[None, :]).astype(F32)
    offsets = facts[groups][None] - 0.5 * facts[:groups]
    offsets = lax.dot_general(offsets, own_hot, (((0,), (1,)), ((), ())), precision=HIGHEST)
    class_hot = (facts[groups + 1][:, None] == jnp.arange(NCLASS, dtype=F32)[None, :]).astype(BF16)
    s2a, s2b, offsets, class_hot = hold((s2a, s2b, offsets, class_hot))

    turn = (y >> 1) ^ (x & 1)
    order = (2 * turn + ((y & 1) ^ turn)).astype(jnp.int32).reshape(1)
    own = []
    for n in (0, 2):
        scores = product(order, (s0, s1, s2a, s2b, s3), gathered, n, 2)
        to3 = lax.ppermute(scores[2][:cols], "x", flip(3))
        to1 = lax.ppermute(scores[2][cols:], "x", flip(1))
        part1 = jnp.concatenate([scores[1][:cols] + to3, scores[1][cols:]], 0)
        part3 = jnp.concatenate([scores[3][:cols], scores[3][cols:] + to1], 0)
        here = scores[0] + offsets[n * cols : (n + 2) * cols]
        own.append(here + lax.ppermute(part1, "x", flip(1)) + lax.ppermute(part3, "x", flip(3)))

    own = jnp.concatenate(own, 0)
    top = jnp.max(own, axis=0)
    terms = jnp.concatenate(split3(jnp.exp(own - top[None])), 1)
    class_part = lax.dot_general(class_hot, terms, FIRST, preferred_element_type=F32)
    class_part = class_part[:, :quarter] + class_part[:, quarter : 2 * quarter] + class_part[:, 2 * quarter :]
    payload = jnp.concatenate([class_part, jnp.broadcast_to(top[None], (8, quarter))], axis=0)
    near = [payload] + [swap_y(payload, step) for step in (1, 2, 3)]
    payload = jnp.stack([lax.select_n(y ^ place, *near) for place in range(4)])
    tops = payload[:, NCLASS]
    row_top = jnp.max(tops, axis=0)
    mass = jnp.sum(payload[:, :NCLASS] * jnp.exp(tops - row_top[None])[:, None, :], axis=0)
    whole = jnp.sum(mass, axis=0)
    evidence = row_top + jnp.log(whole)
    posterior = mass / whole[None]

    counts_here = jnp.pad(jnp.sum(posterior, axis=1), (0, 2 * quarter - NCLASS))
    sent = jnp.concatenate(
        [
            posterior.astype(BF16),
            jnp.stack(split3(evidence)),
            jnp.concatenate([piece.reshape(2, quarter) for piece in split3(counts_here)]),
            jnp.zeros((7, quarter), BF16),
        ],
        0,
    )
    come = jnp.stack([sent] + [lax.ppermute(sent, "h", flip(s)) for s in (1, 2, 3)])
    come = [pick(come, x ^ h ^ p) for p in range(4)]
    weights = jnp.concatenate([piece[:NCLASS] for piece in come], 1)
    log_evidence = jnp.concatenate([jnp.sum(piece[NCLASS : NCLASS + 3].astype(F32), axis=0) for piece in come])
    counts_part = jnp.zeros((2, quarter), F32)
    for piece in come:
        piece = piece[NCLASS + 3 : NCLASS + 9].astype(F32)
        counts_part = counts_part + (piece[:2] + piece[2:4] + piece[4:])
    counts_part = counts_part.reshape(2 * quarter)

    owned = NCLASS // 16
    weights = weights.reshape(8, 2, owned, rows)
    count_row = jnp.pad(counts_part, (0, width - 2 * quarter))

    def sums_of(core):
        kept = jnp.pad(lax.dynamic_index_in_dim(weights, core, 1, False), ((0, 0), (0, 4), (0, 0)))
        sums = jnp.dot(kept.reshape(8 * (owned + 4), rows), images, preferred_element_type=F32)
        sums = sums.reshape(8, owned + 4, width)
        place = lax.broadcasted_iota(jnp.int32, sums.shape, 1)
        return jnp.where(place == owned, count_row[None, None], sums)

    outgoing = sums_of(c) + swap_core(sums_of(1 - c))
    place = lax.broadcasted_iota(jnp.int32, outgoing.shape, 1)
    pieces = [piece[:, owned : owned + 1].astype(F32) for piece in split3(outgoing)]
    for n in (1, 2):
        outgoing = jnp.where(place == owned + n, pieces[n], outgoing)
    arrived = lax.all_to_all(outgoing.astype(BF16), ("a", "x"), 0, 0, tiled=True).astype(F32)
    arrived = jnp.sum(arrived, axis=0)
    counts = jnp.sum(arrived[owned : owned + 3, :NCLASS], axis=0)
    own_counts = lax.dynamic_slice_in_dim(counts, img_place * owned, owned, 0)
    class_avg = arrived[:owned] / (own_counts[:, None] + 1.0)
    occupancy = counts * (NCLASS / (rows * 16))
    return class_avg, occupancy, log_evidence


def solution(mesh):
    split = Mesh(mesh.devices.reshape(2, 4, 2, 4, 4), ("a", "x", "c", "h", "y"))
    img, ref = ("a", "x", "c"), ("h", "y")
    placed = (P(img, ref), P(ref, img), P(), P(img), P(ref), P(ref), P(), P())
    return jax.shard_map(
        body,
        mesh=split,
        in_specs=placed,
        out_specs=(P(img, ref), P(), P(img)),
        check_vma=False,
    )
```
